768 devices in a mesh: dp: 12 (over z), tensor: 8 (over y), pipe: 8 (over x, core).
Axes of the slice: x: 4, y: 8, z: 12, core: 2. Of those that a mesh axis runs over, the one named last changes fastest.
Arguments:
- old_weight: float32 [36864, 4096], P(('dp', 'pipe'), 'tensor'), may hold values from -6 to 6
- old_first_moment: float32 [36864, 4096], P(('dp', 'pipe'), 'tensor'), may hold values from -1.8 to 1.8
- old_second_moment: float32 [36864, 4096], P(('dp', 'pipe'), 'tensor'), may hold values from 0.1 to 2
- gradient: bfloat16 [24576, 4096], P(('dp', 'pipe'), 'tensor'), may hold values from -6 to 6
- hidden: bfloat16 [24576, 3072], P(('dp', 'pipe')), may hold values from -0.15625 to 0.15625
- residual: bfloat16 [3072, 4096], P(('dp', 'pipe'), 'tensor'), may hold values from -64 to 64
- norm_gain: float32 [4096], P('tensor'), may hold values from 0.1 to 1.9
- old_starts: int32 [97], replicated, may hold values from 0 to 112, as said below
- new_starts: int32 [97], replicated, may hold values from 0 to 112, as said below
Outputs:
- new_weight: float32 [24576, 4096], P(('dp', 'pipe'), 'tensor')
- new_first_moment: float32 [24576, 4096], P(('dp', 'pipe'), 'tensor')
- new_second_moment: float32 [24576, 4096], P(('dp', 'pipe'), 'tensor')
- layer_out: bfloat16 [3072, 4096], P(('dp', 'pipe'), 'tensor')
The draws below stay inside these ranges and needn't reach their ends.
Inputs may be any that keep to these rules, and one draw needn't show every extreme that they name: Data index d owns blocks new_starts[d] to new_starts[d+1] - 1, between 1 and 2 of them, and 2 for some index; new_starts begins at 0 and ends at 112. Block slots past a device's count in gradient and hidden are not part of the data. Data index d held blocks old_starts[d] to old_starts[d+1] - 1, at most 3 of them and 3 for some index; an index d with d % 4 == 3 held none, every other index at least one. The new owner of every block is its old holder or the next data index; the blocks that a holder hands to the next index are that index's first blocks, at most 2 of them, and 2 for some index. old_starts begins at 0 and ends at 112. Block slots past a holder's count are not part of the data.
All inputs are finite; a program needn't handle non-finite values.
Results may differ from the reference program's by a relative error of at most 0.0035.
Values sent between devices are 32-bit elements; how exact they have to be, the bound alone decides.
No kernel may reach another device: no remote copies, remote signals or barrier semaphores. Data moves between devices by JAX's collectives and lax.ppermute only.
A program may use at most 64 MiB of HBM per device.

```python
import math
import jax
import jax.numpy as jnp
from jax import lax

D = 4096
FF = 14336
BLOCK_ROWS = 128
STEP = 20
BLOCKS = 112
NEW_CAP = 2
OLD_CAP = 3
TOKENS = 3072
N_DP = 12
N_PIPE = 8


def boundaries(key):
    devices_all = N_DP * N_PIPE
    base_count = BLOCKS // devices_all
    extra_count = BLOCKS - base_count * devices_all
    moved_count = max(4, devices_all // 4) if extra_count == 0 else 0
    slot_cap = OLD_CAP
    device_ids = jnp.arange(devices_all, dtype=jnp.int32)
    scores = jax.random.randint(jax.random.fold_in(key, 11), (devices_all,), 0, 1 << 20)
    scores = jnp.where(device_ids < 4, -1, scores) * devices_all + device_ids
    ranking = jnp.argsort(scores, stable=True).astype(jnp.int32)
    places = jnp.zeros((devices_all,), jnp.int32).at[ranking].set(device_ids)
    counts = base_count + (places < extra_count + moved_count).astype(jnp.int32) - (places >= devices_all - moved_count).astype(jnp.int32)
    quartets = counts.reshape(-1, 4)
    first_count = quartets[:, 0]
    second_count = quartets[:, 1]
    third_count = quartets[:, 2]
    fourth_count = quartets[:, 3]
    groups = quartets.shape[0]
    mid_low = jnp.maximum(0, third_count + fourth_count - slot_cap)
    mid_high = jnp.minimum(jnp.minimum(third_count, third_count + fourth_count - 1), 2 * slot_cap - first_count - second_count)
    pass_mid = jax.random.randint(jax.random.fold_in(key, 12), (groups,), mid_low, mid_high + 1)
    low_low = jnp.maximum(0, second_count + pass_mid - slot_cap)
    low_high = jnp.minimum(jnp.minimum(slot_cap - first_count, second_count), second_count + pass_mid - 1)
    pass_low = jax.random.randint(jax.random.fold_in(key, 13), (groups,), low_low, low_high + 1)
    held = jnp.stack([first_count + pass_low, second_count - pass_low + pass_mid, third_count - pass_mid + fourth_count, jnp.zeros_like(first_count)], axis=1).reshape(-1)
    zero_head = jnp.zeros((1,), jnp.int32)
    new_bounds = jnp.concatenate([zero_head, jnp.cumsum(counts).astype(jnp.int32)])
    old_bounds = jnp.concatenate([zero_head, jnp.cumsum(held).astype(jnp.int32)])
    return (old_bounds.astype(jnp.int32), new_bounds.astype(jnp.int32))


def draw_old_starts(key, part):
    return boundaries(key)[0]


def draw_new_starts(key, part):
    return boundaries(key)[1]


def draw_residual(key, part):
    key = jax.random.fold_in(key, 5)
    base_key, row_key, column_key = jax.random.split(key, 3)
    row_scale = jnp.exp(jax.random.uniform(row_key, (TOKENS, 1), jnp.float32, math.log(0.3), math.log(3.0)))
    column_scale = jnp.exp(jax.random.uniform(column_key, (1, D), jnp.float32, math.log(0.3), math.log(3.0)))
    column_ids = jnp.arange(D, dtype=jnp.float32)[None, :]
    trend = jnp.sqrt(1.0 + 2.0 * column_ids / D)
    values = jnp.clip(jax.random.normal(base_key, (TOKENS, D), jnp.float32), -4.0, 4.0)
    return (values * row_scale * column_scale * trend).astype(jnp.bfloat16)


def spiked(values, stream_key, source, target, parts, factor):
    owner, partner = [(jnp.arange(values.shape[position]) // (values.shape[position] // parts)).reshape([-1 if axis == position else 1 for axis in range(values.ndim)]) for position in (source, target)]
    chosen = jax.random.permutation(stream_key, parts)[partner]
    strong = (owner == chosen) | (owner == (partner + parts // 2) % parts)
    return jnp.where(strong, factor * values, values)


def block_scale(own_key, extent, shards, least, largest):
    gain = 1.0
    for dim, blocks in shards:
        steps = jax.random.uniform(jax.random.fold_in(jax.random.fold_in(own_key, 6), dim), (blocks,), jnp.float32, least / len(shards), largest / len(shards))
        gain = gain * jnp.repeat(jnp.exp(steps), extent[dim] // blocks).reshape((-1,) + (1,) * (len(extent) - 1 - dim))
    return gain


def centred(key, extent, spread, reach, shards=(), kind=jnp.bfloat16):
    factor_of = block_scale(key, extent, shards, -0.22, 0.18) if shards else 1.0
    result = jax.random.normal(key, extent, jnp.float32) * spread * factor_of
    return jnp.minimum(jnp.maximum(result, -reach), reach).astype(kind)


def heavy_noise(rng, shape, width, bound, cuts, heavy, kind=jnp.bfloat16):
    array = width * jax.random.normal(rng, shape, jnp.float32)
    if cuts:
        array = array * block_scale(rng, shape, cuts, -0.22, 0.18)
    return jnp.clip(spiked(array, jax.random.fold_in(rng, 3), *heavy), -bound, bound).astype(kind)


def setup_inputs(seed: int = 0) -> dict:
    key_list = jax.random.split(jax.random.key(seed), 10)
    old_weight = centred(key_list[0], (N_DP * N_PIPE * OLD_CAP * BLOCK_ROWS, D), 1.0, 6.0, ((0, 96), (1, 8)), jnp.float32)
    old_first_moment = centred(key_list[1], (N_DP * N_PIPE * OLD_CAP * BLOCK_ROWS, D), 0.3, 1.8, ((0, 96), (1, 8)), jnp.float32)
    old_second_moment = jnp.clip(jnp.exp(math.log(2.0) - 2.9957323 * jax.random.uniform(key_list[2], (N_DP * N_PIPE * OLD_CAP * BLOCK_ROWS, D), jnp.float32) ** block_scale(key_list[2], (N_DP * N_PIPE * OLD_CAP * BLOCK_ROWS, D), ((0, 96), (1, 8)), -0.2, 0.2)), 0.1, 2.0)
    gradient = centred(key_list[3], (N_DP * N_PIPE * NEW_CAP * BLOCK_ROWS, D), 1.0, 6.0, ((0, 96), (1, 8)))
    hidden = heavy_noise(key_list[4], (N_DP * N_PIPE * NEW_CAP * BLOCK_ROWS, TOKENS), FF ** -0.5, 0.15625, ((0, 96),), (0, 1, 96, 4.75))
    residual = draw_residual(jax.random.fold_in(key_list[9], 71), 0)
    norm_gain = jnp.clip(1.0 + 0.18 * jax.random.normal(key_list[6], (D,), jnp.float32), 0.1, 1.9)
    old_starts = draw_old_starts(jax.random.fold_in(key_list[9], 71), 0)
    new_starts = draw_new_starts(jax.random.fold_in(key_list[9], 71), 0)
    return dict(old_weight=old_weight, old_first_moment=old_first_moment, old_second_moment=old_second_moment, gradient=gradient, hidden=hidden, residual=residual, norm_gain=norm_gain, old_starts=old_starts, new_starts=new_starts)


decay_first = 0.9
decay_second = 0.95
learn_rate = 0.05
weight_decay = 0.1
adam_eps = 1e-08
norm_eps = 1e-05

def owners(starts, number):
    block_ids = jnp.arange(number, dtype=jnp.int32)
    head_list = starts[:-1].astype(jnp.int32)
    owner_ids = lax.optimization_barrier(jnp.sum((head_list[None, :] <= block_ids[:, None]).astype(jnp.int32), axis=1)).astype(jnp.int32) - 1
    slot_ids = block_ids - jnp.take(head_list, owner_ids)
    return (owner_ids.astype(jnp.int32), slot_ids.astype(jnp.int32))

def assemble(source, block_index):
    blocks = source.reshape(-1, BLOCK_ROWS, source.shape[1])
    return jnp.take(blocks, block_index, axis=0).reshape(BLOCKS * BLOCK_ROWS, source.shape[1])

def spread_out(full, block_index):
    blocks = full.reshape(BLOCKS, BLOCK_ROWS, full.shape[1])
    empty = jnp.zeros((N_DP * N_PIPE * NEW_CAP, BLOCK_ROWS, full.shape[1]), jnp.float32)
    return empty.at[block_index].set(blocks).reshape(-1, full.shape[1])

def reference(old_weight, old_first_moment, old_second_moment, gradient, hidden, residual, norm_gain, old_starts, new_starts):
    holder_ids, old_slots = owners(old_starts, BLOCKS)
    owner_ids, new_slots = owners(new_starts, BLOCKS)
    old_index = (holder_ids * OLD_CAP + old_slots).astype(jnp.int32)
    new_index = (owner_ids * NEW_CAP + new_slots).astype(jnp.int32)
    weight = assemble(old_weight, old_index)
    first_moment = assemble(old_first_moment, old_index)
    second_moment = assemble(old_second_moment, old_index)
    grad_full = assemble(gradient, new_index).astype(jnp.float32)
    acts_full = assemble(hidden, new_index)
    first_new = decay_first * first_moment + (1.0 - decay_first) * grad_full
    second_new = decay_second * second_moment + (1.0 - decay_second) * grad_full * grad_full
    corr_first = 1.0 - decay_first ** STEP
    corr_second = 1.0 - decay_second ** STEP
    step_dir = first_new / corr_first / (jnp.sqrt(second_new / corr_second) + adam_eps)
    weight_next = weight - learn_rate * (step_dir + weight_decay * weight)
    weight_half = weight_next.astype(jnp.bfloat16)
    projection = jnp.dot(acts_full.T, weight_half, preferred_element_type=jnp.float32)
    summed = residual.astype(jnp.float32) + projection
    mean_square = lax.optimization_barrier(jnp.mean(summed * summed, axis=1, keepdims=True))
    layer_out = (summed * lax.rsqrt(mean_square + norm_eps) * norm_gain[None, :]).astype(jnp.bfloat16)
    return (spread_out(weight_next, new_index), spread_out(first_new, new_index), spread_out(second_new, new_index), layer_out)
```

```python
import functools

import jax
import jax.numpy as jnp
from jax import lax
from jax.experimental import pallas as pl
from jax.experimental.pallas import tpu as pltpu
from jax.sharding import PartitionSpec as P

BLOCK_ROWS = 128
STEP = 20
SEAT = 32

decay_first = 0.9
decay_second = 0.95
learn_rate = 0.05
weight_decay = 0.1
adam_eps = 1e-08
norm_eps = 1e-05
corr_first = 1.0 - decay_first**STEP
corr_second = 1.0 - decay_second**STEP

DATA = ("dp", "pipe")
F32 = jnp.float32
BF16 = jnp.bfloat16
MIB = 1024 * 1024
COST = pl.CostEstimate(flops=0, bytes_accessed=1024, transcendentals=0)


def params(mib=32):
    return pltpu.CompilerParams(vmem_limit_bytes=mib * MIB)


def clip(value, low, high):
    return jnp.minimum(jnp.maximum(value, low), high)


def send_slot(pos, old_starts, new_starts):
    return clip(new_starts[pos + 1] - old_starts[pos], 0, 1)


def arrival_slot(lane, pos, old_starts, new_starts):
    before = jnp.maximum(pos - 1, 0)
    first = new_starts[pos] - old_starts[before]
    return clip(first - clip(first, 0, 1) + lane, 0, 1)


def kept_slot(lane, pos, old_starts, new_starts):
    return clip(new_starts[pos] + lane - old_starts[pos], 0, 2)


def take_kernel(pos, old_starts, new_starts, *refs):
    sources, out, held, arrivals, departures = refs[:3], *refs[3:]
    slot = send_slot(pos[0], old_starts, new_starts)
    into, onto = [], []
    for i, source in enumerate(sources):
        for lane in range(2):
            there = pl.multiple_of((slot + lane) * BLOCK_ROWS, BLOCK_ROWS)
            here = pl.ds(lane * BLOCK_ROWS, BLOCK_ROWS)
            into.append(
                pltpu.make_async_copy(
                    source.at[pl.ds(there, BLOCK_ROWS), :],
                    held.at[i, here, :],
                    arrivals.at[i, lane],
                )
            )
            onto.append(
                pltpu.make_async_copy(
                    held.at[i, here, :], out.at[i, here, :], departures.at[i, lane]
                )
            )
    for copy in into:
        copy.start()
    for copy, following in zip(into, onto):
        copy.wait()
        following.start()
    for copy in onto:
        copy.wait()


def take_moved(scalars, olds):
    shape = (3, 2 * BLOCK_ROWS, olds[0].shape[1])
    return pl.pallas_call(
        take_kernel,
        in_specs=[pl.BlockSpec(memory_space=pltpu.SMEM)] * 3
        + [pl.BlockSpec(memory_space=pltpu.HBM)] * 3,
        out_specs=pl.BlockSpec(memory_space=pltpu.HBM),
        out_shape=jax.ShapeDtypeStruct(shape, F32),
        scratch_shapes=[
            pltpu.VMEM(shape, F32),
            pltpu.SemaphoreType.DMA((3, 2)),
            pltpu.SemaphoreType.DMA((3, 2)),
        ],
        compiler_params=params(63),
        cost_estimate=COST,
        name="take_moved",
    )(*scalars, *olds)


def keep_kernel(pos, old_starts, new_starts, *refs):
    sources, gradient, out, arrivals = refs[:3], refs[3], refs[4], refs[5]
    copies = []
    for lane in range(2):
        slot = kept_slot(lane, pos[0], old_starts, new_starts)
        there = pl.ds(pl.multiple_of(slot * BLOCK_ROWS, BLOCK_ROWS), BLOCK_ROWS)
        here = pl.ds(lane * BLOCK_ROWS, BLOCK_ROWS)
        copies += [
            pltpu.make_async_copy(source.at[there, :], out.at[i, here, :], arrivals.at[lane, i])
            for i, source in enumerate(sources)
        ]
    for copy in copies:
        copy.start()
    out[3] = gradient[...].astype(F32)
    for copy in copies:
        copy.wait()


def keep_own(scalars, olds, gradient):
    return pl.pallas_call(
        keep_kernel,
        in_specs=[pl.BlockSpec(memory_space=pltpu.SMEM)] * 3
        + [pl.BlockSpec(memory_space=pltpu.HBM)] * 3
        + [pl.BlockSpec(memory_space=pltpu.VMEM)],
        out_shape=jax.ShapeDtypeStruct((4, *gradient.shape), F32),
        scratch_shapes=[pltpu.SemaphoreType.DMA((2, 3))],
        compiler_params=params(),
        cost_estimate=COST,
        name="keep_own",
    )(*scalars, *olds, gradient)


def turn_kernel(seats, pos, block, mine, theirs, turned):
    turned[...] = block[...].T
    core = lax.rem(pos[0], 2)
    for x in range(seats):
        seat = 2 * x
        here = pl.multiple_of((seat + core) * SEAT, SEAT)
        there = pl.multiple_of((seat + 1 - core) * SEAT, SEAT)
        mine[0, x, 0] = turned[pl.ds(here, SEAT), :]
        theirs[0, x, 0] = turned[pl.ds(there, SEAT), :].astype(F32)


def turn_hidden(pos, hidden, groups, seats):
    depth = hidden.shape[0]
    span = 2 * seats * SEAT
    hops = groups // 3
    shape = (3, seats, hops, SEAT, depth)

    def place(z, pos):
        far = lax.rem(z - pos[0] // (2 * seats) + groups, groups)
        return lax.rem(far, 3), 0, z // 3, 0, 0

    block = pl.BlockSpec((1, seats, 1, SEAT, depth), place)
    return pl.pallas_call(
        functools.partial(turn_kernel, seats),
        grid_spec=pltpu.PrefetchScalarGridSpec(
            num_scalar_prefetch=1,
            grid=(groups,),
            in_specs=[pl.BlockSpec((depth, span), lambda z, *_: (0, z))],
            out_specs=[block, block],
            scratch_shapes=[pltpu.VMEM((span, depth), BF16)],
        ),
        out_shape=[jax.ShapeDtypeStruct(shape, BF16), jax.ShapeDtypeStruct(shape, F32)],
        compiler_params=params(),
        cost_estimate=COST,
        name="turn_hidden",
    )(pos, hidden)


def adam_kernel(pos, old_starts, new_starts, kept, moved, *refs):
    new_weight, new_first, new_second, sent = refs
    lane = pl.program_id(0)
    here = pos[0]
    block = new_starts[here] + lane
    arrived = block < jnp.minimum(old_starts[here], new_starts[here + 1])
    live = block < new_starts[here + 1]
    weight_old = jnp.where(arrived, moved[0], kept[0])
    first_old = jnp.where(arrived, moved[1], kept[1])
    second_old = jnp.where(arrived, moved[2], kept[2])
    grad = kept[3]
    first_new = decay_first * first_old + (1.0 - decay_first) * grad
    second_new = decay_second * second_old + (1.0 - decay_second) * grad * grad
    step_dir = (first_new / corr_first) / (jnp.sqrt(second_new / corr_second) + adam_eps)
    weight_next = weight_old - learn_rate * (step_dir + weight_decay * weight_old)
    weight_next = jnp.where(live, weight_next, 0.0)
    new_weight[...] = weight_next
    sent[...] = weight_next
    new_first[...] = jnp.where(live, first_new, 0.0)
    new_second[...] = jnp.where(live, second_new, 0.0)


def adam_step(scalars, kept, moved):
    _, rows, columns = kept.shape

    def arrival(lane, pos, old_starts, new_starts):
        return 0, arrival_slot(lane, pos[0], old_starts, new_starts), 0

    block = (BLOCK_ROWS, columns)
    return pl.pallas_call(
        adam_kernel,
        grid_spec=pltpu.PrefetchScalarGridSpec(
            num_scalar_prefetch=3,
            grid=(2,),
            in_specs=[
                pl.BlockSpec((4, *block), lambda lane, *_: (0, lane, 0)),
                pl.BlockSpec((3, *block), arrival),
            ],
            out_specs=[pl.BlockSpec(block, lambda lane, *_: (lane, 0))] * 4,
        ),
        out_shape=[jax.ShapeDtypeStruct((rows, columns), F32)] * 4,
        compiler_params=params(),
        cost_estimate=COST,
        name="adam_step",
    )(*scalars, kept, moved)


def product_kernel(mine, theirs, weight_mine, weight_theirs, half_a, *half_b):
    sides, seats, rows, _ = mine.shape
    width = half_a.shape[2]
    here = weight_mine[...].astype(BF16)
    there = weight_theirs[...].astype(BF16)
    for side in range(sides):
        for x in range(seats):
            value = jnp.dot(mine[side, x], here, preferred_element_type=F32) + jnp.dot(
                theirs[side, x].astype(BF16), there, preferred_element_type=F32
            )
            half_a[x, side * rows : (side + 1) * rows, :] = value[:, :width]
            half_b[side][x] = value[:, width:]


def products(mine, theirs, weight_mine, weight_theirs):
    sides, seats, rows, _ = mine.shape
    width = weight_mine.shape[1] // 2
    return pl.pallas_call(
        product_kernel,
        out_shape=[jax.ShapeDtypeStruct((seats, sides * rows, width), F32)]
        + [jax.ShapeDtypeStruct((seats, rows, width), F32)] * sides,
        compiler_params=params(),
        cost_estimate=COST,
        name="products",
    )(mine, theirs, weight_mine, weight_theirs)


def add_kernel(*refs):
    value = refs[0][...]
    for ref in refs[1:-1]:
        value = value + ref[...]
    refs[-1][...] = value


def add_up(arrays):
    return pl.pallas_call(
        add_kernel,
        out_shape=jax.ShapeDtypeStruct(arrays[0].shape, F32),
        compiler_params=params(),
        cost_estimate=COST,
        name="add_up",
    )(*arrays)


def split_kernel(stack, *outs):
    rows = outs[0].shape[0]
    for i, out in enumerate(outs):
        out[...] = jnp.sum(stack[:, i * rows : (i + 1) * rows, :], axis=0)


def add_and_split(stack, count):
    _, rows, width = stack.shape
    return pl.pallas_call(
        split_kernel,
        out_shape=[jax.ShapeDtypeStruct((rows // count, width), F32)] * count,
        compiler_params=params(),
        cost_estimate=COST,
        name="add_and_split",
    )(stack)


def merge_kernel(stack, *refs):
    arrays, out = refs[:-1], refs[-1]
    width = stack.shape[2]
    for hop in range(out.shape[0]):
        rows = slice(hop * SEAT, (hop + 1) * SEAT)
        out[hop, :, width:] = jnp.sum(stack[:, rows, :], axis=0)
        value = arrays[0][rows, :]
        for array in arrays[1:]:
            value = value + array[rows, :]
        out[hop, :, :width] = value


def add_and_merge(stack, arrays):
    _, rows, width = stack.shape
    return pl.pallas_call(
        merge_kernel,
        out_shape=jax.ShapeDtypeStruct((rows // SEAT, SEAT, 2 * width), F32),
        compiler_params=params(),
        cost_estimate=COST,
        name="add_and_merge",
    )(stack, *arrays)


def total_kernel(residual, parts, summed, squares):
    square = jnp.zeros((SEAT, 128), F32)
    for start in range(0, residual.shape[1], 128):
        columns = slice(start, start + 128)
        value = residual[:, columns].astype(F32) + jnp.sum(parts[:, :, columns], axis=0)
        summed[:, columns] = value
        square = square + value * value
    row = jnp.sum(square.T, axis=0, keepdims=True)
    row = jnp.concatenate([row] * (128 // SEAT), axis=1)
    squares[...] = jnp.broadcast_to(row[None], squares.shape)


def total_up(residual, parts, peers):
    rows, columns = residual.shape
    return pl.pallas_call(
        total_kernel,
        out_shape=[
            jax.ShapeDtypeStruct((rows, columns), F32),
            jax.ShapeDtypeStruct((peers, 8, 128), F32),
        ],
        compiler_params=params(),
        cost_estimate=COST,
        name="total_up",
    )(residual, parts)


def finish_kernel(features, summed, squares, gain, out):
    row = jnp.sum(squares[...], axis=0)
    scale = lax.rsqrt(row / features + norm_eps)
    wide = jnp.concatenate([scale] * 16, axis=0).T[:SEAT]
    for start in range(0, summed.shape[1], 128):
        columns = slice(start, start + 128)
        out[:, columns] = (summed[:, columns] * wide * gain[:, columns]).astype(BF16)


def finish(summed, squares, gain, features):
    return pl.pallas_call(
        functools.partial(finish_kernel, features),
        out_shape=jax.ShapeDtypeStruct(summed.shape, BF16),
        compiler_params=params(),
        cost_estimate=COST,
        name="finish",
    )(summed, squares, gain.reshape(1, -1))


def on_device(
    old_weight,
    old_first_moment,
    old_second_moment,
    gradient,
    hidden,
    residual,
    norm_gain,
    old_starts,
    new_starts,
):
    columns = old_weight.shape[1]
    width = columns // 2
    groups = lax.axis_size("dp")
    lanes = lax.axis_size("pipe")
    peers = lax.axis_size("tensor")
    seats = lanes // 2
    depth = hidden.shape[0]
    features = columns * peers
    pos = jnp.full((1,), lax.axis_index(DATA), jnp.int32)
    scalars = (pos, old_starts, new_starts)
    olds = (old_weight, old_first_moment, old_second_moment)

    hops = groups // 3
    onward = [(p, p + 1) for p in range(lanes) if p % 4 != 3]
    across = [(p, p ^ 1) for p in range(lanes)]

    by_x = [[2 * x + core for x in range(seats)] for core in range(2)]
    by_hop = [[3 * hop + side for hop in range(hops)] for side in range(3)]

    def spread(array, axis, members):
        return lax.all_to_all(array, axis, 0, 0, axis_index_groups=members)

    def along_z(array, distance):
        route = [(z, (z + distance) % groups) for z in range(groups)]
        return lax.ppermute(array, "dp", route)

    moved = take_moved(scalars, olds)
    after, moved = lax.optimization_barrier((pos, moved))
    moved = lax.ppermute(moved, "pipe", onward)
    mine, theirs = turn_hidden(after, hidden, groups, seats)
    theirs = lax.ppermute(theirs, "pipe", across)
    mine = mine.reshape(3, seats, hops * SEAT, depth)
    theirs = theirs.reshape(3, seats, hops * SEAT, depth)
    kept = keep_own((after, old_starts, new_starts), olds, gradient)

    *state, sent = adam_step(scalars, kept, moved)
    received = lax.ppermute(sent, "pipe", across)
    half_a, first_b, plus_b, minus_b = products(mine, theirs, sent, received)
    half_a = spread(half_a, "pipe", by_x)
    plus_b, minus_b = along_z(plus_b, 1), along_z(minus_b, -1)
    half_a, first_b = lax.optimization_barrier((half_a, first_b))
    half_a = add_and_split(half_a, 3)
    half_a = [half_a[0], along_z(half_a[1], 1), along_z(half_a[2], -1)]
    half_b = spread(add_up([first_b, plus_b, minus_b]), "pipe", by_x)
    parts = spread(add_and_merge(half_b, half_a), "dp", by_hop)
    summed, squares = total_up(residual, parts, peers)
    squares = lax.all_to_all(squares, "tensor", 0, 0)
    layer_out = finish(summed, squares, norm_gain, features)
    return (*state, layer_out)


def solution(mesh):
    data = P(DATA, "tensor")
    return jax.shard_map(
        on_device,
        mesh=mesh,
        in_specs=(data, data, data, data, P(DATA, None), data, P("tensor"), P(), P()),
        out_specs=(data, data, data, data),
        check_vma=False,
    )
```

```python
import functools

import jax
import jax.numpy as jnp
from jax import lax
from jax.experimental import pallas as pl
from jax.experimental.pallas import tpu as pltpu
from jax.sharding import PartitionSpec as P

BLOCK_ROWS = 128
STEP = 20
SEAT = 32

decay_first = 0.9
decay_second = 0.95
learn_rate = 0.05
weight_decay = 0.1
adam_eps = 1e-08
norm_eps = 1e-05
corr_first = 1.0 - decay_first**STEP
corr_second = 1.0 - decay_second**STEP

DATA = ("dp", "pipe")
F32 = jnp.float32
BF16 = jnp.bfloat16
MIB = 1024 * 1024
COST = pl.CostEstimate(flops=0, bytes_accessed=1024, transcendentals=0)


def params(mib=32):
    return pltpu.CompilerParams(vmem_limit_bytes=mib * MIB)


def clip(value, low, high):
    return jnp.minimum(jnp.maximum(value, low), high)


def send_slot(pos, old_starts, new_starts):
    return clip(new_starts[pos + 1] - old_starts[pos], 0, 1)


def arrival_slot(lane, pos, old_starts, new_starts):
    before = jnp.maximum(pos - 1, 0)
    first = new_starts[pos] - old_starts[before]
    return clip(first - clip(first, 0, 1) + lane, 0, 1)


def kept_slot(lane, pos, old_starts, new_starts):
    return clip(new_starts[pos] + lane - old_starts[pos], 0, 2)


def take_kernel(pos, old_starts, new_starts, *refs):
    sources, out, held, arrivals, departures = refs[:3], *refs[3:]
    slot = send_slot(pos[0], old_starts, new_starts)
    into, onto = [], []
    for i, source in enumerate(sources):
        for lane in range(2):
            there = pl.multiple_of((slot + lane) * BLOCK_ROWS, BLOCK_ROWS)
            here = pl.ds(lane * BLOCK_ROWS, BLOCK_ROWS)
            into.append(
                pltpu.make_async_copy(
                    source.at[pl.ds(there, BLOCK_ROWS), :],
                    held.at[i, here, :],
                    arrivals.at[i, lane],
                )
            )
            onto.append(
                pltpu.make_async_copy(
                    held.at[i, here, :], out.at[i, here, :], departures.at[i, lane]
                )
            )
    for copy in into:
        copy.start()
    for copy, following in zip(into, onto):
        copy.wait()
        following.start()
    for copy in onto:
        copy.wait()


def take_moved(scalars, olds):
    shape = (3, 2 * BLOCK_ROWS, olds[0].shape[1])
    return pl.pallas_call(
        take_kernel,
        in_specs=[pl.BlockSpec(memory_space=pltpu.SMEM)] * 3
        + [pl.BlockSpec(memory_space=pltpu.HBM)] * 3,
        out_specs=pl.BlockSpec(memory_space=pltpu.HBM),
        out_shape=jax.ShapeDtypeStruct(shape, F32),
        scratch_shapes=[
            pltpu.VMEM(shape, F32),
            pltpu.SemaphoreType.DMA((3, 2)),
            pltpu.SemaphoreType.DMA((3, 2)),
        ],
        compiler_params=params(63),
        cost_estimate=COST,
        name="take_moved",
    )(*scalars, *olds)


def keep_kernel(pos, old_starts, new_starts, *refs):
    sources, gradient, out, arrivals = refs[:3], refs[3], refs[4], refs[5]
    copies = []
    for lane in range(2):
        slot = kept_slot(lane, pos[0], old_starts, new_starts)
        there = pl.ds(pl.multiple_of(slot * BLOCK_ROWS, BLOCK_ROWS), BLOCK_ROWS)
        here = pl.ds(lane * BLOCK_ROWS, BLOCK_ROWS)
        copies += [
            pltpu.make_async_copy(source.at[there, :], out.at[i, here, :], arrivals.at[lane, i])
            for i, source in enumerate(sources)
        ]
    for copy in copies:
        copy.start()
    out[3] = gradient[...].astype(F32)
    for copy in copies:
        copy.wait()


def keep_own(scalars, olds, gradient):
    return pl.pallas_call(
        keep_kernel,
        in_specs=[pl.BlockSpec(memory_space=pltpu.SMEM)] * 3
        + [pl.BlockSpec(memory_space=pltpu.HBM)] * 3
        + [pl.BlockSpec(memory_space=pltpu.VMEM)],
        out_shape=jax.ShapeDtypeStruct((4, *gradient.shape), F32),
        scratch_shapes=[pltpu.SemaphoreType.DMA((2, 3))],
        compiler_params=params(),
        cost_estimate=COST,
        name="keep_own",
    )(*scalars, *olds, gradient)


def turn_kernel(seats, pos, block, mine, theirs, turned):
    turned[...] = block[...].T
    here_x = lax.rem(pos[0], 2 * seats) // 2
    core = lax.rem(pos[0], 2)
    for away in range(seats):
        x = lax.rem(here_x + away, seats)
        seat = 2 * x
        here = pl.multiple_of((seat + core) * SEAT, SEAT)
        there = pl.multiple_of((seat + 1 - core) * SEAT, SEAT)
        mine[0, away, 0] = turned[pl.ds(here, SEAT), :]
        theirs[0, away, 0] = turned[pl.ds(there, SEAT), :].astype(F32)


def turn_hidden(pos, hidden, groups, seats):
    depth = hidden.shape[0]
    span = 2 * seats * SEAT
    hops = groups // 3
    shape = (3, seats, hops, SEAT, depth)

    def place(z, pos):
        far = lax.rem(z - pos[0] // (2 * seats) + groups, groups)
        return lax.rem(far, 3), 0, z // 3, 0, 0

    block = pl.BlockSpec((1, seats, 1, SEAT, depth), place)
    return pl.pallas_call(
        functools.partial(turn_kernel, seats),
        grid_spec=pltpu.PrefetchScalarGridSpec(
            num_scalar_prefetch=1,
            grid=(groups,),
            in_specs=[pl.BlockSpec((depth, span), lambda z, *_: (0, z))],
            out_specs=[block, block],
            scratch_shapes=[pltpu.VMEM((span, depth), BF16)],
        ),
        out_shape=[jax.ShapeDtypeStruct(shape, BF16), jax.ShapeDtypeStruct(shape, F32)],
        compiler_params=params(),
        cost_estimate=COST,
        name="turn_hidden",
    )(pos, hidden)


def adam_kernel(pos, old_starts, new_starts, kept, moved, new_weight, *moments):
    here = pos[0]
    for lane in range(2):
        block = new_starts[here] + lane
        arrived = block < jnp.minimum(old_starts[here], new_starts[here + 1])
        live = block < new_starts[here + 1]
        slot = arrival_slot(lane, here, old_starts, new_starts)
        there = pl.ds(pl.multiple_of(slot * BLOCK_ROWS, BLOCK_ROWS), BLOCK_ROWS)
        rows = slice(lane * BLOCK_ROWS, (lane + 1) * BLOCK_ROWS)
        weight_old = jnp.where(arrived, moved[0, there, :], kept[0, rows, :])
        first_old = jnp.where(arrived, moved[1, there, :], kept[1, rows, :])
        second_old = jnp.where(arrived, moved[2, there, :], kept[2, rows, :])
        grad = kept[3, rows, :]
        first_new = decay_first * first_old + (1.0 - decay_first) * grad
        second_new = decay_second * second_old + (1.0 - decay_second) * grad * grad
        step_dir = (first_new / corr_first) / (jnp.sqrt(second_new / corr_second) + adam_eps)
        weight_next = weight_old - learn_rate * (step_dir + weight_decay * weight_old)
        new_weight[rows, :] = jnp.where(live, weight_next, 0.0)
        if moments:
            new_first, new_second = moments
            new_first[rows, :] = jnp.where(live, first_new, 0.0)
            new_second[rows, :] = jnp.where(live, second_new, 0.0)


def adam_step(scalars, kept, moved, count):
    return pl.pallas_call(
        adam_kernel,
        in_specs=[pl.BlockSpec(memory_space=pltpu.SMEM)] * 3
        + [pl.BlockSpec(memory_space=pltpu.VMEM)] * 2,
        out_shape=[jax.ShapeDtypeStruct(kept.shape[1:], F32)] * count,
        compiler_params=params(),
        cost_estimate=COST,
        name="adam_step",
    )(*scalars, kept, moved)


def product_kernel(mine, theirs, weight_mine, weight_theirs, *outs):
    sides, seats, rows, _ = mine.shape
    halves_a, halves_b = outs[:seats], outs[seats:]
    width = halves_a[0].shape[1]
    here = weight_mine[...].astype(BF16)
    there = weight_theirs[...].astype(BF16)
    for away in range(seats):
        for side in range(sides):
            value = jnp.dot(mine[side, away], here, preferred_element_type=F32) + jnp.dot(
                theirs[side, away].astype(BF16), there, preferred_element_type=F32
            )
            halves_a[away][side * rows : (side + 1) * rows, :] = value[:, :width]
            halves_b[side][away] = value[:, width:]


def products(mine, theirs, weight_mine, weight_theirs):
    sides, seats, rows, _ = mine.shape
    width = weight_mine.shape[1] // 2
    return pl.pallas_call(
        product_kernel,
        out_shape=[jax.ShapeDtypeStruct((sides * rows, width), F32)] * seats
        + [jax.ShapeDtypeStruct((seats, rows, width), F32)] * sides,
        compiler_params=params(),
        cost_estimate=COST,
        name="products",
    )(mine, theirs, weight_mine, weight_theirs)


def add_kernel(pos, *refs):
    out = refs[-1]
    seats = out.shape[0]
    seat = lax.rem(pos[0], 2 * seats) // 2
    for away in range(seats):
        value = refs[0][away]
        for ref in refs[1:-1]:
            value = value + ref[away]
        out[lax.rem(seat + away, seats)] = value


def add_up(pos, arrays):
    return pl.pallas_call(
        add_kernel,
        in_specs=[pl.BlockSpec(memory_space=pltpu.SMEM)]
        + [pl.BlockSpec(memory_space=pltpu.VMEM)] * len(arrays),
        out_shape=jax.ShapeDtypeStruct(arrays[0].shape, F32),
        compiler_params=params(),
        cost_estimate=COST,
        name="add_up",
    )(pos, *arrays)


def split_kernel(count, *refs):
    outs = refs[count:]
    rows = outs[0].shape[0]
    for i, out in enumerate(outs):
        part = slice(i * rows, (i + 1) * rows)
        value = refs[0][part, :]
        for ref in refs[1:count]:
            value = value + ref[part, :]
        out[...] = value


def add_and_split(arrays, count):
    rows, width = arrays[0].shape
    return pl.pallas_call(
        functools.partial(split_kernel, len(arrays)),
        out_shape=[jax.ShapeDtypeStruct((rows // count, width), F32)] * count,
        compiler_params=params(),
        cost_estimate=COST,
        name="add_and_split",
    )(*arrays)


def merge_kernel(*refs):
    arrays, stack, out = refs[:-2], refs[-2], refs[-1]
    width = stack.shape[2]
    for hop in range(out.shape[0]):
        rows = slice(hop * SEAT, (hop + 1) * SEAT)
        out[hop, :, width:] = jnp.sum(stack[:, rows, :], axis=0)
        value = arrays[0][rows, :]
        for array in arrays[1:]:
            value = value + array[rows, :]
        out[hop, :, :width] = value


def add_and_merge(stack, arrays):
    _, rows, width = stack.shape
    return pl.pallas_call(
        merge_kernel,
        out_shape=jax.ShapeDtypeStruct((rows // SEAT, SEAT, 2 * width), F32),
        compiler_params=params(),
        cost_estimate=COST,
        name="add_and_merge",
    )(*arrays, stack)


def total_kernel(residual, parts, summed, squares):
    square = jnp.zeros((SEAT, 128), F32)
    for start in range(0, residual.shape[1], 128):
        columns = slice(start, start + 128)
        value = residual[:, columns].astype(F32) + jnp.sum(parts[:, :, columns], axis=0)
        summed[:, columns] = value
        square = square + value * value
    row = jnp.sum(square.T, axis=0, keepdims=True)
    row = jnp.concatenate([row] * (128 // SEAT), axis=1)
    squares[...] = jnp.broadcast_to(row[None], squares.shape)


def total_up(residual, parts, peers):
    rows, columns = residual.shape
    return pl.pallas_call(
        total_kernel,
        out_shape=[
            jax.ShapeDtypeStruct((rows, columns), F32),
            jax.ShapeDtypeStruct((peers, 1, 128), F32),
        ],
        compiler_params=params(),
        cost_estimate=COST,
        name="total_up",
    )(residual, parts)


def finish_kernel(features, summed, squares, gain, out):
    row = jnp.broadcast_to(jnp.sum(squares[...], axis=0), (8, 128))
    scale = lax.rsqrt(row / features + norm_eps)
    wide = jnp.concatenate([scale] * 16, axis=0).T[:SEAT]
    for start in range(0, summed.shape[1], 128):
        columns = slice(start, start + 128)
        out[:, columns] = (summed[:, columns] * wide * gain[:, columns]).astype(BF16)


def finish(summed, squares, gain, features):
    return pl.pallas_call(
        functools.partial(finish_kernel, features),
        out_shape=jax.ShapeDtypeStruct(summed.shape, BF16),
        compiler_params=params(),
        cost_estimate=COST,
        name="finish",
    )(summed, squares, gain.reshape(1, -1))


def on_device(
    old_weight,
    old_first_moment,
    old_second_moment,
    gradient,
    hidden,
    residual,
    norm_gain,
    old_starts,
    new_starts,
):
    columns = old_weight.shape[1]
    width = columns // 2
    groups = lax.axis_size("dp")
    lanes = lax.axis_size("pipe")
    peers = lax.axis_size("tensor")
    seats = lanes // 2
    depth = hidden.shape[0]
    features = columns * peers
    pos = jnp.full((1,), lax.axis_index(DATA), jnp.int32)
    scalars = (pos, old_starts, new_starts)
    olds = (old_weight, old_first_moment, old_second_moment)

    hops = groups // 3
    onward = [(p, p + 1) for p in range(lanes) if p % 4 != 3]
    across = [(p, p ^ 1) for p in range(lanes)]

    def along_x(array, distance):
        route = [(p, (p + 2 * distance) % lanes) for p in range(lanes)]
        return lax.ppermute(array, "pipe", route)

    by_x = [[2 * x + core for x in range(seats)] for core in range(2)]
    by_hop = [[3 * hop + side for hop in range(hops)] for side in range(3)]

    def spread(array, axis, members):
        return lax.all_to_all(array, axis, 0, 0, axis_index_groups=members)

    def along_z(array, distance):
        route = [(z, (z + distance) % groups) for z in range(groups)]
        return lax.ppermute(array, "dp", route)

    moved = take_moved(scalars, olds)
    after, moved = lax.optimization_barrier((pos, moved))
    moved = lax.ppermute(moved, "pipe", onward)
    mine, theirs = turn_hidden(after, hidden, groups, seats)
    theirs = lax.ppermute(theirs, "pipe", across)
    mine = mine.reshape(3, seats, hops * SEAT, depth)
    theirs = theirs.reshape(3, seats, hops * SEAT, depth)
    kept = keep_own((after, old_starts, new_starts), olds, gradient)

    (sent,) = adam_step(scalars, kept, moved, 1)
    received = lax.ppermute(sent, "pipe", across)
    state = adam_step(scalars, kept, moved, 3)
    mine, *state = lax.optimization_barrier((mine, *state))
    *half_a, first_b, plus_b, minus_b = products(mine, theirs, sent, received)
    plus_b, minus_b = along_z(plus_b, 1), along_z(minus_b, -1)
    half_a = [half_a[0], *(along_x(half_a[away], away) for away in (2, 1, 3))]
    half_b = spread(add_up(pos, [first_b, plus_b, minus_b]), "pipe", by_x)
    half_a = add_and_split(half_a, 3)
    half_a = [half_a[0], along_z(half_a[1], 1), along_z(half_a[2], -1)]
    parts = spread(add_and_merge(half_b, half_a), "dp", by_hop)
    summed, squares = total_up(residual, parts, peers)
    squares = lax.all_to_all(squares, "tensor", 0, 0)
    layer_out = finish(summed, squares, norm_gain, features)
    return (*state, layer_out)


def solution(mesh):
    data = P(DATA, "tensor")
    return jax.shard_map(
        on_device,
        mesh=mesh,
        in_specs=(data, data, data, data, P(DATA, None), data, P("tensor"), P(), P()),
        out_specs=(data, data, data, data),
        check_vma=False,
    )
```

```python
import functools

import jax
import jax.numpy as jnp
from jax import lax
from jax.experimental import pallas as pl
from jax.experimental.pallas import tpu as pltpu
from jax.sharding import PartitionSpec as P

BLOCK_ROWS = 128
STEP = 20
SEAT = 32

decay_first = 0.9
decay_second = 0.95
learn_rate = 0.05
weight_decay = 0.1
adam_eps = 1e-08
norm_eps = 1e-05
corr_first = 1.0 - decay_first**STEP
corr_second = 1.0 - decay_second**STEP

DATA = ("dp", "pipe")
F32 = jnp.float32
BF16 = jnp.bfloat16
MIB = 1024 * 1024
COST = pl.CostEstimate(flops=0, bytes_accessed=1024, transcendentals=0)


def params(mib=32):
    return pltpu.CompilerParams(vmem_limit_bytes=mib * MIB)


def clip(value, low, high):
    return jnp.minimum(jnp.maximum(value, low), high)


def send_slot(pos, old_starts, new_starts):
    return clip(new_starts[pos + 1] - old_starts[pos], 0, 1)


def arrival_slot(lane, pos, old_starts, new_starts):
    before = jnp.maximum(pos - 1, 0)
    first = new_starts[pos] - old_starts[before]
    return clip(first - clip(first, 0, 1) + lane, 0, 1)


def kept_slot(lane, pos, old_starts, new_starts):
    return clip(new_starts[pos] + lane - old_starts[pos], 0, 2)


def take_kernel(pos, old_starts, new_starts, *refs):
    sources, out, held, arrivals, departures = refs[:3], *refs[3:]
    slot = send_slot(pos[0], old_starts, new_starts)
    into, onto = [], []
    for i, source in enumerate(sources):
        for lane in range(2):
            there = pl.multiple_of((slot + lane) * BLOCK_ROWS, BLOCK_ROWS)
            here = pl.ds(lane * BLOCK_ROWS, BLOCK_ROWS)
            into.append(
                pltpu.make_async_copy(
                    source.at[pl.ds(there, BLOCK_ROWS), :],
                    held.at[i, here, :],
                    arrivals.at[i, lane],
                )
            )
            onto.append(
                pltpu.make_async_copy(
                    held.at[i, here, :], out.at[i, here, :], departures.at[i, lane]
                )
            )
    for copy in into:
        copy.start()
    for copy, following in zip(into, onto):
        copy.wait()
        following.start()
    for copy in onto:
        copy.wait()


def take_moved(scalars, olds):
    shape = (3, 2 * BLOCK_ROWS, olds[0].shape[1])
    return pl.pallas_call(
        take_kernel,
        in_specs=[pl.BlockSpec(memory_space=pltpu.SMEM)] * 3
        + [pl.BlockSpec(memory_space=pltpu.HBM)] * 3,
        out_specs=pl.BlockSpec(memory_space=pltpu.HBM),
        out_shape=jax.ShapeDtypeStruct(shape, F32),
        scratch_shapes=[
            pltpu.VMEM(shape, F32),
            pltpu.SemaphoreType.DMA((3, 2)),
            pltpu.SemaphoreType.DMA((3, 2)),
        ],
        compiler_params=params(63),
        cost_estimate=COST,
        name="take_moved",
    )(*scalars, *olds)


def keep_kernel(pos, old_starts, new_starts, *refs):
    sources, gradient, out, arrivals = refs[:3], refs[3], refs[4], refs[5]
    copies = []
    for lane in range(2):
        slot = kept_slot(lane, pos[0], old_starts, new_starts)
        there = pl.ds(pl.multiple_of(slot * BLOCK_ROWS, BLOCK_ROWS), BLOCK_ROWS)
        here = pl.ds(lane * BLOCK_ROWS, BLOCK_ROWS)
        copies += [
            pltpu.make_async_copy(source.at[there, :], out.at[i, here, :], arrivals.at[lane, i])
            for i, source in enumerate(sources)
        ]
    for copy in copies:
        copy.start()
    out[3] = gradient[...].astype(F32)
    for copy in copies:
        copy.wait()


def keep_own(scalars, olds, gradient):
    return pl.pallas_call(
        keep_kernel,
        in_specs=[pl.BlockSpec(memory_space=pltpu.SMEM)] * 3
        + [pl.BlockSpec(memory_space=pltpu.HBM)] * 3
        + [pl.BlockSpec(memory_space=pltpu.VMEM)],
        out_shape=jax.ShapeDtypeStruct((4, *gradient.shape), F32),
        scratch_shapes=[pltpu.SemaphoreType.DMA((2, 3))],
        compiler_params=params(),
        cost_estimate=COST,
        name="keep_own",
    )(*scalars, *olds, gradient)


def turn_kernel(seats, pos, block, mine, theirs, turned):
    turned[...] = block[...].T
    here_x = lax.rem(pos[0], 2 * seats) // 2
    core = lax.rem(pos[0], 2)
    for away in range(seats):
        x = lax.rem(here_x + away, seats)
        seat = 2 * x
        here = pl.multiple_of((seat + core) * SEAT, SEAT)
        there = pl.multiple_of((seat + 1 - core) * SEAT, SEAT)
        mine[0, away, 0] = turned[pl.ds(here, SEAT), :]
        theirs[0, away, 0] = turned[pl.ds(there, SEAT), :].astype(F32)


def turn_hidden(pos, hidden, groups, seats):
    depth = hidden.shape[0]
    span = 2 * seats * SEAT
    hops = groups // 3
    shape = (3, seats, hops, SEAT, depth)

    def place(z, pos):
        far = lax.rem(z - pos[0] // (2 * seats) + groups, groups)
        return lax.rem(far, 3), 0, z // 3, 0, 0

    block = pl.BlockSpec((1, seats, 1, SEAT, depth), place)
    return pl.pallas_call(
        functools.partial(turn_kernel, seats),
        grid_spec=pltpu.PrefetchScalarGridSpec(
            num_scalar_prefetch=1,
            grid=(groups,),
            in_specs=[pl.BlockSpec((depth, span), lambda z, *_: (0, z))],
            out_specs=[block, block],
            scratch_shapes=[pltpu.VMEM((span, depth), BF16)],
        ),
        out_shape=[jax.ShapeDtypeStruct(shape, BF16), jax.ShapeDtypeStruct(shape, F32)],
        compiler_params=params(),
        cost_estimate=COST,
        name="turn_hidden",
    )(pos, hidden)


def adam_kernel(pos, old_starts, new_starts, kept, moved, *refs):
    here = pos[0]
    for lane in range(2):
        block = new_starts[here] + lane
        arrived = block < jnp.minimum(old_starts[here], new_starts[here + 1])
        live = block < new_starts[here + 1]
        slot = arrival_slot(lane, here, old_starts, new_starts)
        there = pl.ds(pl.multiple_of(slot * BLOCK_ROWS, BLOCK_ROWS), BLOCK_ROWS)
        rows = slice(lane * BLOCK_ROWS, (lane + 1) * BLOCK_ROWS)
        weight_old = jnp.where(arrived, moved[0, there, :], kept[0, rows, :])
        first_old = jnp.where(arrived, moved[1, there, :], kept[1, rows, :])
        second_old = jnp.where(arrived, moved[2, there, :], kept[2, rows, :])
        grad = kept[3, rows, :]
        first_new = decay_first * first_old + (1.0 - decay_first) * grad
        second_new = decay_second * second_old + (1.0 - decay_second) * grad * grad
        if len(refs) > 1:
            sent, new_weight, new_first, new_second = refs
            new_weight[rows, :] = sent[rows, :]
            new_first[rows, :] = jnp.where(live, first_new, 0.0)
            new_second[rows, :] = jnp.where(live, second_new, 0.0)
            continue
        step_dir = (first_new / corr_first) / (jnp.sqrt(second_new / corr_second) + adam_eps)
        weight_next = weight_old - learn_rate * (step_dir + weight_decay * weight_old)
        refs[0][rows, :] = jnp.where(live, weight_next, 0.0)


def adam_step(scalars, kept, moved, *sent):
    count = 3 if sent else 1
    return pl.pallas_call(
        adam_kernel,
        in_specs=[pl.BlockSpec(memory_space=pltpu.SMEM)] * 3
        + [pl.BlockSpec(memory_space=pltpu.VMEM)] * (2 + len(sent)),
        out_shape=[jax.ShapeDtypeStruct(kept.shape[1:], F32)] * count,
        compiler_params=params(),
        cost_estimate=COST,
        name="adam_step",
    )(*scalars, kept, moved, *sent)


def product_kernel(mine, theirs, weight_mine, weight_theirs, *outs):
    sides, seats, rows, _ = mine.shape
    halves_a, halves_b = outs[:seats], outs[seats:]
    width = halves_a[0].shape[1]
    here = weight_mine[...].astype(BF16)
    there = weight_theirs[...].astype(BF16)
    for away in range(seats):
        for side in range(sides):
            value = jnp.dot(mine[side, away], here, preferred_element_type=F32) + jnp.dot(
                theirs[side, away].astype(BF16), there, preferred_element_type=F32
            )
            halves_a[away][side * rows : (side + 1) * rows, :] = value[:, :width]
            halves_b[side][away] = value[:, width:]


def products(mine, theirs, weight_mine, weight_theirs):
    sides, seats, rows, _ = mine.shape
    width = weight_mine.shape[1] // 2
    return pl.pallas_call(
        product_kernel,
        out_shape=[jax.ShapeDtypeStruct((sides * rows, width), F32)] * seats
        + [jax.ShapeDtypeStruct((seats, rows, width), F32)] * sides,
        compiler_params=params(),
        cost_estimate=COST,
        name="products",
    )(mine, theirs, weight_mine, weight_theirs)


def add_kernel(pos, *refs):
    out = refs[-1]
    seats = out.shape[0]
    seat = lax.rem(pos[0], 2 * seats) // 2
    for away in range(seats):
        value = refs[0][away]
        for ref in refs[1:-1]:
            value = value + ref[away]
        out[lax.rem(seat + away, seats)] = value


def add_up(pos, arrays):
    return pl.pallas_call(
        add_kernel,
        in_specs=[pl.BlockSpec(memory_space=pltpu.SMEM)]
        + [pl.BlockSpec(memory_space=pltpu.VMEM)] * len(arrays),
        out_shape=jax.ShapeDtypeStruct(arrays[0].shape, F32),
        compiler_params=params(),
        cost_estimate=COST,
        name="add_up",
    )(pos, *arrays)


def split_kernel(count, *refs):
    outs = refs[count:]
    rows = outs[0].shape[0]
    for i, out in enumerate(outs):
        part = slice(i * rows, (i + 1) * rows)
        value = refs[0][part, :]
        for ref in refs[1:count]:
            value = value + ref[part, :]
        out[...] = value


def add_and_split(arrays, count):
    rows, width = arrays[0].shape
    return pl.pallas_call(
        functools.partial(split_kernel, len(arrays)),
        out_shape=[jax.ShapeDtypeStruct((rows // count, width), F32)] * count,
        compiler_params=params(),
        cost_estimate=COST,
        name="add_and_split",
    )(*arrays)


def merge_kernel(*refs):
    arrays, stack, out = refs[:-2], refs[-2], refs[-1]
    width = stack.shape[2]
    for hop in range(out.shape[0]):
        rows = slice(hop * SEAT, (hop + 1) * SEAT)
        out[hop, :, width:] = jnp.sum(stack[:, rows, :], axis=0)
        value = arrays[0][rows, :]
        for array in arrays[1:]:
            value = value + array[rows, :]
        out[hop, :, :width] = value


def add_and_merge(stack, arrays):
    _, rows, width = stack.shape
    return pl.pallas_call(
        merge_kernel,
        out_shape=jax.ShapeDtypeStruct((rows // SEAT, SEAT, 2 * width), F32),
        compiler_params=params(),
        cost_estimate=COST,
        name="add_and_merge",
    )(*arrays, stack)


def total_kernel(residual, parts, summed, squares):
    square = jnp.zeros((SEAT, 128), F32)
    for start in range(0, residual.shape[1], 128):
        columns = slice(start, start + 128)
        value = residual[:, columns].astype(F32) + jnp.sum(parts[:, :, columns], axis=0)
        summed[:, columns] = value
        square = square + value * value
    row = jnp.sum(square.T, axis=0, keepdims=True)
    row = jnp.concatenate([row] * (128 // SEAT), axis=1)
    squares[...] = jnp.broadcast_to(row[None], squares.shape)


def total_up(residual, parts, peers):
    rows, columns = residual.shape
    return pl.pallas_call(
        total_kernel,
        out_shape=[
            jax.ShapeDtypeStruct((rows, columns), F32),
            jax.ShapeDtypeStruct((peers, 1, 128), F32),
        ],
        compiler_params=params(),
        cost_estimate=COST,
        name="total_up",
    )(residual, parts)


def finish_kernel(features, summed, squares, gain, out):
    row = jnp.broadcast_to(jnp.sum(squares[...], axis=0), (8, 128))
    scale = lax.rsqrt(row / features + norm_eps)
    wide = jnp.concatenate([scale] * 16, axis=0).T[:SEAT]
    for start in range(0, summed.shape[1], 128):
        columns = slice(start, start + 128)
        out[:, columns] = (summed[:, columns] * wide * gain[:, columns]).astype(BF16)


def finish(summed, squares, gain, features):
    return pl.pallas_call(
        functools.partial(finish_kernel, features),
        out_shape=jax.ShapeDtypeStruct(summed.shape, BF16),
        compiler_params=params(),
        cost_estimate=COST,
        name="finish",
    )(summed, squares, gain.reshape(1, -1))


def on_device(
    old_weight,
    old_first_moment,
    old_second_moment,
    gradient,
    hidden,
    residual,
    norm_gain,
    old_starts,
    new_starts,
):
    columns = old_weight.shape[1]
    width = columns // 2
    groups = lax.axis_size("dp")
    lanes = lax.axis_size("pipe")
    peers = lax.axis_size("tensor")
    seats = lanes // 2
    depth = hidden.shape[0]
    features = columns * peers
    pos = jnp.full((1,), lax.axis_index(DATA), jnp.int32)
    scalars = (pos, old_starts, new_starts)
    olds = (old_weight, old_first_moment, old_second_moment)

    hops = groups // 3
    onward = [(p, p + 1) for p in range(lanes) if p % 4 != 3]
    across = [(p, p ^ 1) for p in range(lanes)]

    def along_x(array, distance):
        route = [(p, (p + 2 * distance) % lanes) for p in range(lanes)]
        return lax.ppermute(array, "pipe", route)

    by_x = [[2 * x + core for x in range(seats)] for core in range(2)]
    by_hop = [[3 * hop + side for hop in range(hops)] for side in range(3)]

    def spread(array, axis, members):
        return lax.all_to_all(array, axis, 0, 0, axis_index_groups=members)

    def along_z(array, distance):
        route = [(z, (z + distance) % groups) for z in range(groups)]
        return lax.ppermute(array, "dp", route)

    moved = take_moved(scalars, olds)
    after, moved = lax.optimization_barrier((pos, moved))
    moved = lax.ppermute(moved, "pipe", onward)
    mine, theirs = turn_hidden(after, hidden, groups, seats)
    theirs = lax.ppermute(theirs, "pipe", across)
    mine = mine.reshape(3, seats, hops * SEAT, depth)
    theirs = theirs.reshape(3, seats, hops * SEAT, depth)
    kept = keep_own((after, old_starts, new_starts), olds, gradient)

    (sent,) = adam_step(scalars, kept, moved)
    received = lax.ppermute(sent, "pipe", across)
    state = adam_step(scalars, kept, moved, sent)
    mine, *state = lax.optimization_barrier((mine, *state))
    *half_a, first_b, plus_b, minus_b = products(mine, theirs, sent, received)
    plus_b, minus_b = along_z(plus_b, 1), along_z(minus_b, -1)
    half_a = [half_a[0], *(along_x(half_a[away], away) for away in (2, 1, 3))]
    half_b = spread(add_up(pos, [first_b, plus_b, minus_b]), "pipe", by_x)
    half_a = add_and_split(half_a, 3)
    half_a = [half_a[0], along_z(half_a[1], 1), along_z(half_a[2], -1)]
    parts = spread(add_and_merge(half_b, half_a), "dp", by_hop)
    summed, squares = total_up(residual, parts, peers)
    squares = lax.all_to_all(squares, "tensor", 0, 0)
    layer_out = finish(summed, squares, norm_gain, features)
    return (*state, layer_out)


def solution(mesh):
    data = P(DATA, "tensor")
    return jax.shard_map(
        on_device,
        mesh=mesh,
        in_specs=(data, data, data, data, P(DATA, None), data, P("tensor"), P(), P()),
        out_specs=(data, data, data, data),
        check_vma=False,
    )
```
